512 devices in a mesh: section: 16 (over z), seq: 32 (over y, x, core).
Axes of the slice: x: 4, y: 4, z: 16, core: 2. Of those that a mesh axis runs over, the one named last changes fastest.
Arguments:
- fresh: bfloat16 [16, 512, 3, 4096], P('section', 'seq'), may hold values from -16 to 16
- stale: bfloat16 [16, 16, 512, 2, 4096], P('section', None, None, None, 'seq'), may hold values from -6 to 6
- section_patch: int32 [16], P('section'), may hold values from 0 to 15, as said below
Outputs:
- handed: bfloat16 [16, 512, 4096], P('section', 'seq')
The draws below stay inside these ranges and needn't reach their ends.
Inputs may be any that keep to these rules, and one draw needn't show every extreme that they name: section_patch[s] = (t - s) mod 16 for a plan offset t, so each patch is at exactly one section.
All inputs are finite; a program needn't handle non-finite values.
Results may differ from the reference program's by a relative error of at most 0.0048.
Values may be sent and summed in bfloat16 or wider, within the bound.
No kernel may reach another device: no remote copies, remote signals or barrier semaphores. Data moves between devices by JAX's collectives and lax.ppermute only.
A program may use at most 128 MiB of HBM per device.

```python
import jax
import jax.numpy as jnp
from jax import lax

HD = 128
HEADS = 32
PATCH = 512
SECTIONS = 16
PATCHES = 16


def draw_fresh(key, part):
    key = jax.random.fold_in(key, 1)
    shape = (SECTIONS, PATCH, 3, HEADS * HD)
    base = jnp.clip(jax.random.normal(key, shape, jnp.float32), -4.0, 4.0)
    return base.astype(jnp.bfloat16)


def draw_section_patch(key, part):
    key = jax.random.fold_in(key, 2)
    offset = jax.random.randint(key, (), 0, SECTIONS, dtype=jnp.int32)
    sections = jnp.arange(SECTIONS, dtype=jnp.int32)
    return (offset - sections) % SECTIONS


def block_levels(stream_key, dims, shards, low, high):
    factor_of = 1.0
    for position, shards_of in shards:
        steps = jax.random.uniform(jax.random.fold_in(jax.random.fold_in(stream_key, 6), position), (shards_of,), jnp.float32, low / len(shards), high / len(shards))
        factor_of = factor_of * jnp.repeat(jnp.exp(steps), dims[position] // shards_of).reshape((-1,) + (1,) * (len(dims) - 1 - position))
    return factor_of


def centred(rng, shape, spread, bound, shards=(), kind=jnp.bfloat16):
    drawn = jax.random.normal(rng, shape, jnp.float32) * spread
    if len(shards) > 0:
        drawn = block_levels(rng, shape, shards, -0.22, 0.18) * drawn
    return jnp.clip(drawn, min=-bound, max=bound).astype(kind)


def setup_inputs(seed: int = 0) -> dict:
    key_of = jax.random.split(jax.random.key(seed), 4)
    return {
        "fresh": draw_fresh(jax.random.fold_in(key_of[3], 71), 0),
        "stale": centred(key_of[1], (SECTIONS, PATCHES, PATCH, 2, HEADS * HD), 1.0, 6.0, ((0, 16), (4, 32))),
        "section_patch": draw_section_patch(jax.random.fold_in(key_of[3], 71), 0),
    }


def attend_head(args):
    queries, keys, values = args
    scale = HD ** -0.5
    scores = jnp.dot(queries.astype(jnp.float32), keys.astype(jnp.float32).T) * scale
    expo = jnp.exp(scores - jnp.max(scores, axis=-1, keepdims=True))
    total = jnp.sum(expo, axis=-1, keepdims=True)
    weights = expo.astype(jnp.bfloat16)
    summed = jnp.dot(weights.astype(jnp.float32), values.astype(jnp.float32))
    return (summed / total).astype(jnp.bfloat16)


def per_section(args):
    fresh_section, stale_section, own = args
    slots = jnp.arange(PATCHES, dtype=jnp.int32)
    keep = (slots == own)[:, None, None, None]
    keyval = jnp.where(keep, fresh_section[None, :, 1:3, :], stale_section)
    keyval = keyval.reshape(PATCHES * PATCH, 2, HEADS, HD)
    queries = fresh_section[:, 0, :].reshape(PATCH, HEADS, HD).transpose(1, 0, 2)
    keys = keyval[:, 0].transpose(1, 0, 2)
    values = keyval[:, 1].transpose(1, 0, 2)
    out = lax.map(attend_head, (queries, keys, values))
    return out.transpose(1, 0, 2).reshape(PATCH, HEADS * HD)


def reference(fresh, stale, section_patch):
    attended = lax.map(per_section, (fresh, stale, section_patch))
    return jnp.roll(attended, 1, axis=0)
```

```python
import functools
import math

import jax
import jax.numpy as jnp
from jax import lax
from jax.experimental import pallas as pl
from jax.experimental.pallas import tpu as pltpu
from jax.sharding import PartitionSpec as P

HD = 128
FACTOR = HD**-0.5 * math.log2(math.e)


def attend_kernel(chunk, own_ref, qkv_ref, keys_ref, values_ref, out_ref):
    devices, rows, width = qkv_ref.shape
    tokens = rows // 3
    patch = devices * tokens
    count = keys_ref.shape[0] // chunk
    own = own_ref[0]

    def received(part):
        return qkv_ref[:, part * tokens : (part + 1) * tokens, :].reshape(patch, width)

    scaled = received(0).astype(jnp.float32) * FACTOR
    high = scaled.astype(jnp.bfloat16)
    low = (scaled - high.astype(jnp.float32)).astype(jnp.bfloat16)
    queries = jnp.concatenate([high, low], axis=1)
    new_keys = received(1)
    new_values = received(2)
    ones = jnp.ones((chunk, width), jnp.bfloat16)

    def block(ref, fresh, index):
        pieces = []
        for part in range(chunk // patch):
            slot = index * (chunk // patch) + part
            piece = ref[slot * patch : (slot + 1) * patch, :]
            pieces.append(jnp.where(own == slot, fresh, piece))
        return jnp.concatenate(pieces, axis=0)

    def score(index):
        keys = block(keys_ref, new_keys, index)
        keys = jnp.concatenate([keys, keys], axis=1)
        return lax.dot_general(
            queries, keys, (((1,), (1,)), ((), ())), preferred_element_type=jnp.float32
        )

    top = None
    summed = None
    scores = score(0)
    for index in range(count):
        later = score(index + 1) if index + 1 < count else None
        peak = jnp.max(scores, axis=1, keepdims=True)
        new_top = peak if top is None else jnp.maximum(top, peak)
        weights = jnp.exp2(scores - new_top).astype(jnp.bfloat16)
        values = jnp.concatenate([block(values_ref, new_values, index), ones], axis=1)
        term = jnp.dot(weights, values, preferred_element_type=jnp.float32)
        summed = term if top is None else summed * jnp.exp2(top - new_top) + term
        top = new_top
        scores = later
    out = summed[:, :width] / summed[:, width:]
    out_ref[...] = out.astype(jnp.bfloat16).reshape(out_ref.shape)


def attend(own, qkv, keys, values):
    devices, rows, width = qkv.shape
    tokens = rows // 3
    length = keys.shape[0]
    patch = devices * tokens
    vmem = pl.BlockSpec(memory_space=pltpu.VMEM)
    return pl.pallas_call(
        functools.partial(attend_kernel, 2 * patch),
        out_shape=jax.ShapeDtypeStruct((devices, tokens, width), jnp.bfloat16),
        in_specs=[pl.BlockSpec(memory_space=pltpu.SMEM), vmem, vmem, vmem],
        out_specs=vmem,
        compiler_params=pltpu.CompilerParams(vmem_limit_bytes=32 << 20),
        cost_estimate=pl.CostEstimate(
            flops=4 * patch * length * width,
            bytes_accessed=4 * length * width,
            transcendentals=patch * length,
        ),
        name="attend",
    )(own, qkv, keys, values)


def body(fresh, stale, section_patch):
    _, tokens, parts, total_width = fresh.shape
    _, slots, patch, _, width = stale.shape
    devices = lax.axis_size("seq")
    sections = lax.axis_size("section")

    packed = fresh[0].reshape(tokens, parts, devices, width)
    packed = packed.transpose(2, 1, 0, 3).reshape(devices, parts * tokens, width)
    qkv = lax.all_to_all(packed, "seq", split_axis=0, concat_axis=0, tiled=True)

    cache = stale[0].reshape(slots * patch, 2, width)
    attended = attend(section_patch, qkv, cache[:, 0], cache[:, 1])

    pairs = [(source, (source + 1) % sections) for source in range(sections)]
    handed = lax.ppermute(attended, "section", pairs)
    handed = lax.all_to_all(handed, "seq", split_axis=0, concat_axis=0, tiled=True)
    return handed.transpose(1, 0, 2).reshape(1, tokens, total_width)


def solution(mesh):
    return jax.shard_map(
        body,
        mesh=mesh,
        in_specs=(
            P("section", "seq", None, None),
            P("section", None, None, None, "seq"),
            P("section"),
        ),
        out_specs=P("section", "seq", None),
        check_vma=False,
    )
```

```python
import functools
import math

import jax
import jax.numpy as jnp
from jax import lax
from jax.experimental import pallas as pl
from jax.experimental.pallas import tpu as pltpu
from jax.sharding import PartitionSpec as P

HD = 128
CHUNK = 1024
FACTOR = HD**-0.5 * math.log2(math.e)


def attend_kernel(
    chunk, own_ref, qkv_ref, keys_ref, front_ref, back_hbm, out_ref, back_ref,
    weights_ref, decay_ref, summed_ref, sem
):
    devices, rows, width = qkv_ref.shape
    tokens = rows // 3
    patch = devices * tokens
    count = keys_ref.shape[0] // chunk
    half = front_ref.shape[0]
    own = own_ref[0]
    fetch = pltpu.make_async_copy(back_hbm, back_ref, sem)
    fetch.start()

    def received(part):
        return qkv_ref[:, part * tokens : (part + 1) * tokens, :].reshape(patch, width)

    scaled = received(0).astype(jnp.float32) * FACTOR
    high = scaled.astype(jnp.bfloat16)
    low = (scaled - high.astype(jnp.float32)).astype(jnp.bfloat16)
    queries = jnp.concatenate([high, low], axis=1)
    new_keys = received(1)
    new_values = received(2)
    ones = jnp.ones((chunk, width), jnp.bfloat16)

    def block(ref, first, fresh, index):
        pieces = []
        for start in range(index * chunk, (index + 1) * chunk, patch):
            piece = ref[start - first : start - first + patch, :]
            pieces.append(jnp.where(own == start // patch, fresh, piece))
        return jnp.concatenate(pieces, axis=0)

    def score(index):
        keys = block(keys_ref, 0, new_keys, index)
        keys = jnp.concatenate([keys, keys], axis=1)
        return lax.dot_general(
            queries, keys, (((1,), (1,)), ((), ())), preferred_element_type=jnp.float32
        )

    def accumulate(summed, weights, decay, values):
        values = jnp.concatenate([values, ones], axis=1)
        term = jnp.dot(weights, values, preferred_element_type=jnp.float32)
        return term if summed is None else summed * decay + term

    @pl.when(own >= 0)
    def first():
        top = None
        decay = None
        summed = None
        scores = score(0)
        for index in range(count):
            later = score(index + 1) if index + 1 < count else None
            peak = jnp.max(scores, axis=1, keepdims=True)
            new_top = peak if top is None else jnp.maximum(top, peak)
            weights = jnp.exp2(scores - new_top).astype(jnp.bfloat16)
            if top is not None:
                decay = jnp.exp2(top - new_top)
            if index * chunk < half:
                values = block(front_ref, 0, new_values, index)
                summed = accumulate(summed, weights, decay, values)
            else:
                weights_ref[index - half // chunk] = weights
                decay_ref[index - half // chunk] = jnp.broadcast_to(decay, (patch, width))
            top = new_top
            scores = later
        summed_ref[...] = summed

    fetch.wait()
    summed = summed_ref[...]
    for index in range(half // chunk, count):
        values = block(back_ref, half, new_values, index)
        decay = decay_ref[index - half // chunk]
        decay = jnp.concatenate([decay, decay], axis=1)
        summed = accumulate(summed, weights_ref[index - half // chunk], decay, values)
    out = summed[:, :width] / summed[:, width:]
    out_ref[...] = out.astype(jnp.bfloat16).reshape(out_ref.shape)


def attend(own, qkv, keys, front, back):
    devices, rows, width = qkv.shape
    tokens = rows // 3
    length = keys.shape[0]
    patch = devices * tokens
    vmem = pl.BlockSpec(memory_space=pltpu.VMEM)
    return pl.pallas_call(
        functools.partial(attend_kernel, CHUNK),
        out_shape=jax.ShapeDtypeStruct((devices, tokens, width), jnp.bfloat16),
        in_specs=[
            pl.BlockSpec(memory_space=pltpu.SMEM),
            vmem,
            vmem,
            vmem,
            pl.BlockSpec(memory_space=pltpu.HBM),
        ],
        out_specs=vmem,
        scratch_shapes=[
            pltpu.VMEM(back.shape, back.dtype),
            pltpu.VMEM((length // CHUNK // 2, patch, CHUNK), jnp.bfloat16),
            pltpu.VMEM((length // CHUNK // 2, patch, width), jnp.float32),
            pltpu.VMEM((patch, 2 * width), jnp.float32),
            pltpu.SemaphoreType.DMA,
        ],
        compiler_params=pltpu.CompilerParams(vmem_limit_bytes=36 << 20),
        cost_estimate=pl.CostEstimate(
            flops=4 * patch * length * width,
            bytes_accessed=4 * length * width,
            transcendentals=patch * length,
        ),
        name="attend",
    )(own, qkv, keys, front, back)


def body(fresh, stale, section_patch):
    _, tokens, parts, total_width = fresh.shape
    _, slots, patch, _, width = stale.shape
    devices = lax.axis_size("seq")
    sections = lax.axis_size("section")

    packed = fresh[0].reshape(tokens // 8, 8, parts, devices, width)
    packed = packed.transpose(3, 2, 0, 1, 4).reshape(devices, parts * tokens, width)
    qkv = lax.all_to_all(packed, "seq", split_axis=0, concat_axis=0, tiled=True)

    cache = stale[0].reshape(slots * patch, 2, width)
    half = slots // 2 * patch
    keys, front, back = cache[:, 0], cache[:half, 1], cache[half:, 1]
    back = pltpu.with_memory_space_constraint(back, pltpu.HBM)
    attended = attend(section_patch, qkv, keys, front, back)

    pairs = [(source, (source + 1) % sections) for source in range(sections)]
    handed = lax.ppermute(attended, "section", pairs)
    handed = lax.all_to_all(handed, "seq", split_axis=0, concat_axis=0, tiled=True)
    handed = handed.reshape(devices, tokens // 8, 8, width).transpose(1, 2, 0, 3)
    return handed.reshape(1, tokens, total_width)


def solution(mesh):
    return jax.shard_map(
        body,
        mesh=mesh,
        in_specs=(
            P("section", "seq", None, None),
            P("section", None, None, None, "seq"),
            P("section"),
        ),
        out_specs=P("section", "seq", None),
        check_vma=False,
    )
```

```python
import functools
import math

import jax
import jax.numpy as jnp
from jax import lax
from jax.experimental import pallas as pl
from jax.experimental.pallas import tpu as pltpu
from jax.sharding import PartitionSpec as P

HD = 128
CHUNK = 2048
FACTOR = HD**-0.5 * math.log2(math.e)


def attend_kernel(
    chunk, own_ref, qkv_ref, keys_ref, front_ref, back_hbm, out_ref, back_ref,
    scores_ref, top_ref, sem
):
    devices, rows, width = qkv_ref.shape
    tokens = rows // 3
    patch = devices * tokens
    count = keys_ref.shape[0] // chunk
    half = front_ref.shape[0]
    own = own_ref[0]
    fetch = pltpu.make_async_copy(back_hbm, back_ref, sem)
    fetch.start()

    def received(part):
        return qkv_ref[:, part * tokens : (part + 1) * tokens, :].reshape(patch, width)

    queries = received(0)
    new_keys = received(1)
    new_values = received(2)
    ones = jnp.ones((chunk, width), jnp.bfloat16)

    def block(ref, first, fresh, index):
        pieces = []
        for start in range(index * chunk, (index + 1) * chunk, patch):
            piece = ref[start - first : start - first + patch, :]
            if ref is not back_ref:
                piece = jnp.where(own == start // patch, fresh, piece)
            pieces.append(piece)
        return jnp.concatenate(pieces, axis=0)

    def score(index):
        keys = block(keys_ref, 0, new_keys, index)
        return lax.dot_general(
            queries, keys, (((1,), (1,)), ((), ())), preferred_element_type=jnp.float32
        )

    def accumulate(summed, weights, decay, values):
        values = jnp.concatenate([values, ones], axis=1)
        term = jnp.dot(weights, values, preferred_element_type=jnp.float32)
        if summed is None:
            return term
        return (summed if decay is None else summed * decay) + term

    held = half // chunk

    @pl.when(own >= 0)
    def first():
        top = None
        for index in range(held):
            scores = score(index)
            scores_ref[index] = scores
            peak = jnp.max(scores, axis=1, keepdims=True)
            top = peak if top is None else jnp.maximum(top, peak)
        top_ref[...] = jnp.broadcast_to(top, (patch, width))

    fetch.wait()

    @pl.when(own >= half // patch)
    def replace():
        start = pl.multiple_of(own * patch - half, patch)
        back_ref[pl.ds(start, patch), :] = new_values

    top = top_ref[:, :1]
    decay = None
    summed = None
    later = []
    for index in range(count):
        if index < held:
            later.append(score(held + index))
            scores = scores_ref[index]
        else:
            scores = later[index - held]
            peak = jnp.max(scores, axis=1, keepdims=True)
            new_top = jnp.maximum(top, peak)
            decay = jnp.exp2((top - new_top) * FACTOR)
            top = new_top
        weights = jnp.exp2((scores - top) * FACTOR).astype(jnp.bfloat16)
        if index < held:
            values = block(front_ref, 0, new_values, index)
        else:
            values = block(back_ref, half, new_values, index)
        summed = accumulate(summed, weights, decay, values)
    out = summed[:, :width] / summed[:, width:]
    out_ref[...] = out.astype(jnp.bfloat16).reshape(out_ref.shape)


def attend(own, qkv, keys, front, back):
    devices, rows, width = qkv.shape
    tokens = rows // 3
    length = keys.shape[0]
    patch = devices * tokens
    vmem = pl.BlockSpec(memory_space=pltpu.VMEM)
    return pl.pallas_call(
        functools.partial(attend_kernel, CHUNK),
        out_shape=jax.ShapeDtypeStruct((devices, tokens, width), jnp.bfloat16),
        in_specs=[
            pl.BlockSpec(memory_space=pltpu.SMEM),
            vmem,
            vmem,
            vmem,
            pl.BlockSpec(memory_space=pltpu.HBM),
        ],
        out_specs=vmem,
        scratch_shapes=[
            pltpu.VMEM(back.shape, back.dtype),
            pltpu.VMEM((length // CHUNK // 2, patch, CHUNK), jnp.float32),
            pltpu.VMEM((patch, width), jnp.float32),
            pltpu.SemaphoreType.DMA,
        ],
        compiler_params=pltpu.CompilerParams(vmem_limit_bytes=36 << 20),
        cost_estimate=pl.CostEstimate(
            flops=4 * patch * length * width,
            bytes_accessed=4 * length * width,
            transcendentals=patch * length,
        ),
        name="attend",
    )(own, qkv, keys, front, back)


def body(fresh, stale, section_patch):
    _, tokens, parts, total_width = fresh.shape
    _, slots, patch, _, width = stale.shape
    devices = lax.axis_size("seq")
    sections = lax.axis_size("section")

    packed = fresh[0].reshape(tokens // 8, 8, parts, devices, width)
    packed = packed.transpose(3, 2, 0, 1, 4).reshape(devices, parts * tokens, width)
    qkv = lax.all_to_all(packed, "seq", split_axis=0, concat_axis=0, tiled=True)

    cache = stale[0].reshape(slots * patch, 2, width)
    half = slots // 2 * patch
    keys, front, back = cache[:, 0], cache[:half, 1], cache[half:, 1]
    back = pltpu.with_memory_space_constraint(back, pltpu.HBM)
    attended = attend(section_patch, qkv, keys, front, back)

    pairs = [(source, (source + 1) % sections) for source in range(sections)]
    handed = lax.ppermute(attended, "section", pairs)
    handed = lax.all_to_all(handed, "seq", split_axis=0, concat_axis=0, tiled=True)
    handed = handed.reshape(devices, tokens // 8, 8, width).transpose(1, 2, 0, 3)
    return handed.reshape(1, tokens, total_width)


def solution(mesh):
    return jax.shard_map(
        body,
        mesh=mesh,
        in_specs=(
            P("section", "seq", None, None),
            P("section", None, None, None, "seq"),
            P("section"),
        ),
        out_specs=P("section", "seq", None),
        check_vma=False,
    )
```

```python
import functools
import math

import jax
import jax.numpy as jnp
from jax import lax
from jax.experimental import pallas as pl
from jax.experimental.pallas import tpu as pltpu
from jax.sharding import PartitionSpec as P

HD = 128
CHUNK = 2048
FACTOR = HD**-0.5 * math.log2(math.e)


def attend_kernel(
    chunk, own_ref, qkv_ref, keys_ref, front_ref, back_hbm, out_ref, back_ref,
    scores_ref, top_ref, sem
):
    devices, rows, width = qkv_ref.shape
    tokens = rows // 3
    patch = devices * tokens
    count = keys_ref.shape[0] // chunk
    half = front_ref.shape[0]
    own = own_ref[0]
    fetch = pltpu.make_async_copy(back_hbm, back_ref, sem)
    fetch.start()

    def received(part):
        return qkv_ref[:, part * tokens : (part + 1) * tokens, :].reshape(patch, width)

    queries = received(0)
    new_keys = received(1)
    new_values = received(2)
    ones = jnp.ones((chunk, width), jnp.bfloat16)

    def block(ref, first, fresh, index):
        pieces = []
        for start in range(index * chunk, (index + 1) * chunk, patch):
            piece = ref[start - first : start - first + patch, :]
            if ref is not back_ref:
                piece = jnp.where(own == start // patch, fresh, piece)
            pieces.append(piece)
        return jnp.concatenate(pieces, axis=0)

    def score(index):
        keys = block(keys_ref, 0, new_keys, index)
        return lax.dot_general(
            queries, keys, (((1,), (1,)), ((), ())), preferred_element_type=jnp.float32
        )

    def accumulate(summed, weights, decay, values):
        values = jnp.concatenate([values, ones], axis=1)
        term = jnp.dot(weights, values, preferred_element_type=jnp.float32)
        if summed is None:
            return term
        return (summed if decay is None else summed * decay) + term

    held = half // chunk

    @pl.when(own >= 0)
    def first():
        top = None
        for index in range(held):
            scores = score(index)
            scores_ref[index] = scores
            peak = jnp.max(scores, axis=1, keepdims=True)
            top = peak if top is None else jnp.maximum(top, peak)
        top_ref[...] = jnp.broadcast_to(top, (patch, width))

    fetch.wait()

    @pl.when(own >= half // patch)
    def replace():
        start = pl.multiple_of(own * patch - half, patch)
        back_ref[pl.ds(start, patch), :] = new_values

    top = top_ref[:, :1]
    decay = None
    summed = None
    later = []
    for index in range(count):
        if index < held:
            later.append(score(held + index))
            scores = scores_ref[index]
        else:
            scores = later[index - held]
            peak = jnp.max(scores, axis=1, keepdims=True)
            new_top = jnp.maximum(top, peak)
            decay = jnp.exp2((top - new_top) * FACTOR)
            top = new_top
        weights = jnp.exp2((scores - top) * FACTOR).astype(jnp.bfloat16)
        if index < held:
            values = block(front_ref, 0, new_values, index)
        else:
            values = block(back_ref, half, new_values, index)
        summed = accumulate(summed, weights, decay, values)
    out = summed[:, :width] / summed[:, width:]
    out_ref[...] = out.astype(jnp.bfloat16).reshape(out_ref.shape)


def attend(own, qkv, keys, front, back):
    devices, rows, width = qkv.shape
    tokens = rows // 3
    length = keys.shape[0]
    patch = devices * tokens
    vmem = pl.BlockSpec(memory_space=pltpu.VMEM)
    return pl.pallas_call(
        functools.partial(attend_kernel, CHUNK),
        out_shape=jax.ShapeDtypeStruct((devices, tokens, width), jnp.bfloat16),
        in_specs=[
            pl.BlockSpec(memory_space=pltpu.SMEM),
            vmem,
            vmem,
            vmem,
            pl.BlockSpec(memory_space=pltpu.HBM),
        ],
        out_specs=vmem,
        scratch_shapes=[
            pltpu.VMEM(back.shape, back.dtype),
            pltpu.VMEM((length // CHUNK // 2, patch, CHUNK), jnp.float32),
            pltpu.VMEM((patch, width), jnp.float32),
            pltpu.SemaphoreType.DMA,
        ],
        compiler_params=pltpu.CompilerParams(vmem_limit_bytes=36 << 20),
        cost_estimate=pl.CostEstimate(
            flops=4 * patch * length * width,
            bytes_accessed=4 * length * width,
            transcendentals=patch * length,
        ),
        name="attend",
    )(own, qkv, keys, front, back)


def body(fresh, stale, section_patch):
    _, tokens, parts, total_width = fresh.shape
    _, slots, patch, _, width = stale.shape
    devices = lax.axis_size("seq")
    sections = lax.axis_size("section")

    packed = fresh[0].reshape(tokens // 8, 8, parts, devices, width)
    packed = packed.transpose(3, 2, 0, 1, 4).reshape(devices, parts * tokens, width)
    qkv = lax.all_to_all(packed, "seq", split_axis=0, concat_axis=0, tiled=True)

    cache = stale[0].reshape(slots * patch, 2, width)
    half = slots // 2 * patch
    keys, front, back = cache[:, 0], cache[:half, 1], cache[half:, 1]
    back = pltpu.with_memory_space_constraint(back, pltpu.HBM)
    attended = attend(section_patch, qkv, keys, front, back)

    handed = lax.all_to_all(attended, "seq", split_axis=0, concat_axis=0, tiled=True)
    handed = handed.reshape(devices, tokens // 8, 8, width).transpose(1, 2, 0, 3)
    handed = handed.reshape(1, tokens, total_width)
    pairs = [(source, (source + 1) % sections) for source in range(sections)]
    return lax.ppermute(handed, "section", pairs)


def solution(mesh):
    return jax.shard_map(
        body,
        mesh=mesh,
        in_specs=(
            P("section", "seq", None, None),
            P("section", None, None, None, "seq"),
            P("section"),
        ),
        out_specs=P("section", "seq", None),
        check_vma=False,
    )
```

```python
import functools
import math

import jax
import jax.numpy as jnp
from jax import lax
from jax.experimental import pallas as pl
from jax.experimental.pallas import tpu as pltpu
from jax.sharding import PartitionSpec as P

HD = 128
CHUNK = 2048
FACTOR = HD**-0.5 * math.log2(math.e)


def attend_kernel(
    chunk, own_ref, qkv_ref, keys_ref, front_ref, back_hbm, out_ref, back_ref,
    scores_ref, top_ref, sem
):
    devices, rows, width = qkv_ref.shape
    tokens = rows // 3
    patch = devices * tokens
    count = keys_ref.shape[0] // chunk
    half = front_ref.shape[0]
    own = own_ref[0]
    fetch = pltpu.make_async_copy(back_hbm, back_ref, sem)
    fetch.start()

    def received(part):
        return qkv_ref[:, part * tokens : (part + 1) * tokens, :].reshape(patch, width)

    queries = received(0)
    new_keys = received(1)
    new_values = received(2)
    ones = jnp.ones((chunk, width), jnp.bfloat16)

    def block(ref, first, fresh, index):
        pieces = []
        for start in range(index * chunk, (index + 1) * chunk, patch):
            piece = ref[start - first : start - first + patch, :]
            if ref is not back_ref:
                piece = jnp.where(own == start // patch, fresh, piece)
            pieces.append(piece)
        return jnp.concatenate(pieces, axis=0)

    def score(index):
        keys = block(keys_ref, 0, new_keys, index)
        return lax.dot_general(
            queries, keys, (((1,), (1,)), ((), ())), preferred_element_type=jnp.float32
        )

    def accumulate(summed, weights, decay, values):
        values = jnp.concatenate([values, ones], axis=1)
        term = jnp.dot(weights, values, preferred_element_type=jnp.float32)
        if summed is None:
            return term
        return (summed if decay is None else summed * decay) + term

    held = half // chunk

    @pl.when(own >= 0)
    def first():
        top = None
        for index in range(held):
            scores = score(index)
            scores_ref[index] = scores
            peak = jnp.max(scores, axis=1, keepdims=True)
            top = peak if top is None else jnp.maximum(top, peak)
        top_ref[...] = jnp.broadcast_to(top, (patch, width))

    fetch.wait()

    @pl.when(own >= half // patch)
    def replace():
        start = pl.multiple_of(own * patch - half, patch)
        back_ref[pl.ds(start, patch), :] = new_values

    top = top_ref[:, :1]
    decay = None
    summed = None
    later = []
    for index in range(count):
        if index == 0:
            later = [score(held + more) for more in range(held)]
        if index < held:
            scores = scores_ref[index]
        else:
            scores = later[index - held]
            peak = jnp.max(scores, axis=1, keepdims=True)
            new_top = jnp.maximum(top, peak)
            decay = jnp.exp2((top - new_top) * FACTOR)
            top = new_top
        weights = jnp.exp2((scores - top) * FACTOR).astype(jnp.bfloat16)
        if index < held:
            values = block(front_ref, 0, new_values, index)
        else:
            values = block(back_ref, half, new_values, index)
        summed = accumulate(summed, weights, decay, values)
    out = summed[:, :width] / summed[:, width:]
    out_ref[...] = out.astype(jnp.bfloat16).reshape(out_ref.shape)


def attend(own, qkv, keys, front, back):
    devices, rows, width = qkv.shape
    tokens = rows // 3
    length = keys.shape[0]
    patch = devices * tokens
    vmem = pl.BlockSpec(memory_space=pltpu.VMEM)
    return pl.pallas_call(
        functools.partial(attend_kernel, CHUNK),
        out_shape=jax.ShapeDtypeStruct((devices, tokens, width), jnp.bfloat16),
        in_specs=[
            pl.BlockSpec(memory_space=pltpu.SMEM),
            vmem,
            vmem,
            vmem,
            pl.BlockSpec(memory_space=pltpu.HBM),
        ],
        out_specs=vmem,
        scratch_shapes=[
            pltpu.VMEM(back.shape, back.dtype),
            pltpu.VMEM((length // CHUNK // 2, patch, CHUNK), jnp.float32),
            pltpu.VMEM((patch, width), jnp.float32),
            pltpu.SemaphoreType.DMA,
        ],
        compiler_params=pltpu.CompilerParams(vmem_limit_bytes=36 << 20),
        cost_estimate=pl.CostEstimate(
            flops=4 * patch * length * width,
            bytes_accessed=4 * length * width,
            transcendentals=patch * length,
        ),
        name="attend",
    )(own, qkv, keys, front, back)


def body(fresh, stale, section_patch):
    _, tokens, parts, total_width = fresh.shape
    _, slots, patch, _, width = stale.shape
    devices = lax.axis_size("seq")
    sections = lax.axis_size("section")

    packed = fresh[0].reshape(tokens // 8, 8, parts, devices, width)
    packed = packed.transpose(3, 2, 0, 1, 4).reshape(devices, parts * tokens, width)
    qkv = lax.all_to_all(packed, "seq", split_axis=0, concat_axis=0, tiled=True)

    cache = stale[0].reshape(slots * patch, 2, width)
    half = slots // 2 * patch
    keys, front, back = cache[:, 0], cache[:half, 1], cache[half:, 1]
    back = pltpu.with_memory_space_constraint(back, pltpu.HBM)
    attended = attend(section_patch, qkv, keys, front, back)

    handed = lax.all_to_all(attended, "seq", split_axis=0, concat_axis=0, tiled=True)
    handed = handed.reshape(devices, tokens // 8, 8, width).transpose(1, 2, 0, 3)
    handed = handed.reshape(1, tokens, total_width)
    pairs = [(source, (source + 1) % sections) for source in range(sections)]
    return lax.ppermute(handed, "section", pairs)


def solution(mesh):
    return jax.shard_map(
        body,
        mesh=mesh,
        in_specs=(
            P("section", "seq", None, None),
            P("section", None, None, None, "seq"),
            P("section"),
        ),
        out_specs=P("section", "seq", None),
        check_vma=False,
    )
```

```python
import functools
import math

import jax
import jax.numpy as jnp
from jax import lax
from jax.experimental import pallas as pl
from jax.experimental.pallas import tpu as pltpu
from jax.sharding import PartitionSpec as P

HD = 128
CHUNK = 2048
FACTOR = HD**-0.5 * math.log2(math.e)


def attend_kernel(
    chunk, own_ref, qkv_ref, keys_ref, front_ref, back_hbm, out_ref, back_ref,
    scores_ref, top_ref, sem
):
    devices, rows, width = qkv_ref.shape
    tokens = rows // 3
    patch = devices * tokens
    count = keys_ref.shape[0] // chunk
    half = front_ref.shape[0]
    own = own_ref[0]
    fetch = pltpu.make_async_copy(back_hbm, back_ref, sem)
    fetch.start()

    def received(part):
        return qkv_ref[:, part * tokens : (part + 1) * tokens, :].reshape(patch, width)

    queries = received(0)
    new_keys = received(1)
    new_values = received(2)
    ones = jnp.ones((chunk, width), jnp.bfloat16)

    def block(ref, first, fresh, index):
        pieces = []
        for start in range(index * chunk, (index + 1) * chunk, patch):
            piece = ref[start - first : start - first + patch, :]
            if ref is not back_ref:
                piece = jnp.where(own == start // patch, fresh, piece)
            pieces.append(piece)
        return jnp.concatenate(pieces, axis=0)

    def score(index):
        keys = block(keys_ref, 0, new_keys, index)
        return lax.dot_general(
            queries, keys, (((1,), (1,)), ((), ())), preferred_element_type=jnp.float32
        )

    def accumulate(summed, weights, decay, values):
        values = jnp.concatenate([values, ones], axis=1)
        term = jnp.dot(weights, values, preferred_element_type=jnp.float32)
        if summed is None:
            return term
        return (summed if decay is None else summed * decay) + term

    held = half // chunk

    @pl.when(own >= 0)
    def first():
        top = None
        for index in range(held):
            scores = score(index)
            scores_ref[index] = scores
            peak = jnp.max(scores, axis=1, keepdims=True)
            top = peak if top is None else jnp.maximum(top, peak)
        top_ref[...] = jnp.broadcast_to(top, (patch, width))

    fetch.wait()

    @pl.when(own >= half // patch)
    def replace():
        start = pl.multiple_of(own * patch - half, patch)
        back_ref[pl.ds(start, patch), :] = new_values

    top = top_ref[:, :1]
    decay = None
    summed = None
    later = []
    for index in range(count):
        if index == 0:
            later = [score(held + more) for more in range(held)]
        if index < held:
            scores = scores_ref[index]
        else:
            scores = later[index - held]
            peak = jnp.max(scores, axis=1, keepdims=True)
            new_top = jnp.maximum(top, peak)
            decay = jnp.exp2((top - new_top) * FACTOR)
            top = new_top
        weights = jnp.exp2((scores - top) * FACTOR).astype(jnp.bfloat16)
        if index < held:
            values = block(front_ref, 0, new_values, index)
        else:
            values = block(back_ref, half, new_values, index)
        summed = accumulate(summed, weights, decay, values)
    out = summed[:, :width] / summed[:, width:]
    out_ref[...] = out.astype(jnp.bfloat16).reshape(out_ref.shape)


def attend(own, qkv, keys, front, back):
    devices, rows, width = qkv.shape
    tokens = rows // 3
    length = keys.shape[0]
    patch = devices * tokens
    vmem = pl.BlockSpec(memory_space=pltpu.VMEM)
    return pl.pallas_call(
        functools.partial(attend_kernel, CHUNK),
        out_shape=jax.ShapeDtypeStruct((devices, tokens, width), jnp.bfloat16),
        in_specs=[
            pl.BlockSpec(memory_space=pltpu.SMEM),
            vmem,
            vmem,
            vmem,
            pl.BlockSpec(memory_space=pltpu.HBM),
        ],
        out_specs=vmem,
        scratch_shapes=[
            pltpu.VMEM(back.shape, back.dtype),
            pltpu.VMEM((length // CHUNK // 2, patch, CHUNK), jnp.float32),
            pltpu.VMEM((patch, width), jnp.float32),
            pltpu.SemaphoreType.DMA,
        ],
        compiler_params=pltpu.CompilerParams(vmem_limit_bytes=36 << 20),
        cost_estimate=pl.CostEstimate(
            flops=4 * patch * length * width,
            bytes_accessed=4 * length * width,
            transcendentals=patch * length,
        ),
        name="attend",
    )(own, qkv, keys, front, back)


def body(fresh, stale, section_patch):
    _, tokens, parts, total_width = fresh.shape
    _, slots, patch, _, width = stale.shape
    devices = lax.axis_size("seq")
    sections = lax.axis_size("section")

    packed = fresh[0].reshape(tokens // 8, 8, parts, devices, width)
    packed = packed.transpose(3, 2, 0, 1, 4).reshape(devices, parts * tokens, width)
    qkv = lax.all_to_all(packed, "seq", split_axis=0, concat_axis=0, tiled=True)

    cache = stale[0].reshape(slots * patch, 2, width)
    half = slots // 2 * patch
    keys, front, back = cache[:, 0], cache[:half, 1], cache[half:, 1]
    back = pltpu.with_memory_space_constraint(back, pltpu.HBM)
    attended = attend(section_patch, qkv, keys, front, back)

    handed = lax.all_to_all(attended, "seq", split_axis=0, concat_axis=0, tiled=True)
    pairs = [(source, (source + 1) % sections) for source in range(sections)]
    handed = lax.ppermute(handed, "section", pairs)
    handed = handed.reshape(devices, tokens // 8, 8, width).transpose(1, 2, 0, 3)
    return handed.reshape(1, tokens, total_width)


def solution(mesh):
    return jax.shard_map(
        body,
        mesh=mesh,
        in_specs=(
            P("section", "seq", None, None),
            P("section", None, None, None, "seq"),
            P("section"),
        ),
        out_specs=P("section", "seq", None),
        check_vma=False,
    )
```
